256 devices in a mesh: dp: 128 (over y_hi, x, z, core), dup: 2 (over y_lo).
Axes of the slice: x: 4, y: 4 (y_hi: 2, y_lo: 2; y = y_hi * 2 + y_lo), z: 8, core: 2. Of those that a mesh axis runs over, the one named last changes fastest.
Arguments:
- visual_embedding_matrix: bfloat16 [131072, 1024], P(('dp', 'dup')), may hold values from -6 to 6
- description_matrix: bfloat16 [131072, 1024], P(('dp', 'dup')), may hold values from -6 to 6
- sharpness_factor: float32 [1], replicated, may hold values from 0.05 to 0.1
Outputs:
- image_loss: float32 [131072], P(('dp', 'dup'))
- text_loss: float32 [131072], P(('dp', 'dup'))
- image_grad: float32 [131072, 1024], P(('dp', 'dup'))
- text_grad: float32 [131072, 1024], P(('dp', 'dup'))
The draws below stay inside these ranges and needn't reach their ends.
All inputs are finite; a program needn't handle non-finite values.
Results may differ from the reference program's by a relative error of at most 0.0014.
Values may be sent and summed in bfloat16 or wider, within the bound.
A program may use at most 128 MiB of HBM per device.

```python
import jax
import jax.numpy as jnp
from jax import lax

E = 1024
BLOCK = 1024
NEIGH = 2
ROWS = 131072
N_DP = 128


def draw_rows(key):
    values = jnp.clip(jax.random.normal(key, (ROWS, E), jnp.float32), -6.0, 6.0)
    return values.astype(jnp.bfloat16)


def draw_visual_embedding_matrix(key, part):
    key = jax.random.fold_in(key, 1)
    return draw_rows(key)


def draw_description_matrix(key, part):
    key = jax.random.fold_in(key, 2)
    return draw_rows(key)


def setup_inputs(seed: int = 0) -> dict:
    key_list = jax.random.split(jax.random.key(seed), 4)
    return {
        "visual_embedding_matrix": draw_visual_embedding_matrix(jax.random.fold_in(key_list[3], 71), 0),
        "description_matrix": draw_description_matrix(jax.random.fold_in(key_list[3], 71), 0),
        "sharpness_factor": jnp.clip(jax.random.uniform(key_list[2], (1,), jnp.float32, 0.05, 0.1), 0.05, 0.1),
    }


def pairwise_logits(left, right, similarity_multiplier):
    return jnp.dot(left, right.T, preferred_element_type=jnp.float32) * similarity_multiplier


def reference(visual_embedding_matrix, description_matrix, sharpness_factor):
    similarity_multiplier = sharpness_factor[0]
    visual_tile_list = visual_embedding_matrix.reshape(N_DP, BLOCK, E)
    txt_blocks = description_matrix.reshape(N_DP, BLOCK, E)
    offsets = jnp.arange(NEIGH + 1, dtype=jnp.int32)
    numbers = jnp.arange(N_DP, dtype=jnp.int32)

    def text_window(block):
        return txt_blocks[(block + offsets) % N_DP].reshape(-1, E)

    def image_span_rows(block):
        return visual_tile_list[(block - offsets) % N_DP].reshape(-1, E)

    def row_pass(block):
        scores = pairwise_logits(visual_tile_list[block], text_window(block), similarity_multiplier)
        return jax.nn.logsumexp(scores, axis=1), jnp.diagonal(scores[:, :BLOCK])

    row_lse, matched_logits = lax.map(row_pass, numbers)

    def col_pass(block):
        scores = pairwise_logits(image_span_rows(block), txt_blocks[block], similarity_multiplier)
        return jax.nn.logsumexp(scores, axis=0)

    caption_normalizer_vector = lax.map(col_pass, numbers)

    def image_part(block):
        block_span = text_window(block)
        scores = pairwise_logits(visual_tile_list[block], block_span, similarity_multiplier)
        col_part = caption_normalizer_vector[(block + offsets) % N_DP].reshape(-1)
        softmax_weights = (jnp.exp(scores - row_lse[block][:, None]) + jnp.exp(scores - col_part[None, :])).astype(jnp.bfloat16)
        summed = jnp.dot(softmax_weights, block_span, preferred_element_type=jnp.float32)
        return similarity_multiplier * summed - 2.0 * similarity_multiplier * txt_blocks[block].astype(jnp.float32)

    def text_part(block):
        block_span = image_span_rows(block)
        scores = pairwise_logits(block_span, txt_blocks[block], similarity_multiplier)
        row_segment = row_lse[(block - offsets) % N_DP].reshape(-1)
        softmax_weights = (jnp.exp(scores - row_segment[:, None]) + jnp.exp(scores - caption_normalizer_vector[block][None, :])).astype(jnp.bfloat16)
        summed = jnp.dot(softmax_weights.T, block_span, preferred_element_type=jnp.float32)
        return similarity_multiplier * summed - 2.0 * similarity_multiplier * visual_tile_list[block].astype(jnp.float32)

    image_grad = lax.map(image_part, numbers).reshape(-1, E)
    text_grad = lax.map(text_part, numbers).reshape(-1, E)
    image_loss = (row_lse - matched_logits).reshape(-1)
    text_loss = (caption_normalizer_vector - matched_logits).reshape(-1)
    return image_loss, text_loss, image_grad, text_grad
```

```python
import functools
import math

import jax
import jax.numpy as jnp
from jax import lax
from jax.experimental import pallas as pl
from jax.experimental.pallas import tpu as pltpu
from jax.sharding import PartitionSpec as P

MESH = pl.DeviceIdType.MESH
LOG2E = math.log2(math.e)
LN2 = math.log(2.0)
CHUNKS = 8
LOW = -1e30

FIRST_EVEN = [
    (0, 0, 0), (0, 0, 1), (1, 2, 0), (2, 2, 1), (4, 1, 0), (4, 4, 0),
    (5, 4, 1), (6, 3, 0), (7, 5, 0), (8, 1, 1), (8, 3, 1), (8, 5, 1),
]
FIRST_ODD = [
    (0, 0, 0), (0, 0, 1), (4, 1, 0), (4, 2, 0), (5, 4, 0), (5, 4, 1),
    (6, 5, 0), (7, 2, 1), (7, 3, 0), (8, 1, 1), (8, 5, 1), (8, 3, 1),
]
SECOND_EVEN = [
    (1, 0, 0), (1, 0, 1), (2, 1, 0), (2, 1, 1), (2, 2, 0), (2, 2, 1),
    (3, 3, 0), (3, 3, 1), (3, 4, 0), (4, 4, 1), (4, 5, 0), (4, 5, 1),
    (4, 6, 0), (5, 6, 1), (5, 8, 0), (5, 8, 1), (5, 10, 0), (6, 10, 1),
    (6, 7, 0), (6, 11, 0), (6, 9, 0), (8, 7, 1), (9, 11, 1), (9, 9, 1),
]
SECOND_ODD = [
    (1, 0, 0), (1, 0, 1), (2, 1, 0), (2, 1, 1), (2, 2, 0), (2, 2, 1),
    (3, 3, 0), (3, 3, 1), (3, 6, 0), (4, 6, 1), (4, 8, 0), (4, 8, 1),
    (4, 10, 0), (5, 10, 1), (5, 4, 0), (5, 4, 1), (5, 5, 0), (6, 7, 0),
    (6, 11, 0), (6, 9, 0), (8, 7, 1), (9, 11, 1), (9, 9, 1), (9, 5, 1),
]


def looked_up(index, odd, even_list, odd_list):
    def words(entries):
        codes = [k * 32 + slot * 2 + part for k, slot, part in entries]
        codes += [0] * (-len(codes) % 3)
        return [sum(c << (9 * i) for i, c in enumerate(codes[at : at + 3])) for at in range(0, len(codes), 3)]

    group = index // 3
    word = jnp.int32(0)
    for at, (even_word, odd_word) in enumerate(zip(words(even_list), words(odd_list))):
        word = jnp.where(group == at, jnp.where(odd == 1, odd_word, even_word), word)
    code = lax.shift_right_logical(word, 9 * (index - group * 3)) & 511
    return code // 32, (code % 32) // 2, code % 2


def wide(column, count):
    return jnp.concatenate([column] * (count // 128), axis=1)


def log2(value):
    return jnp.log(value) * LOG2E


def merged(first, second):
    top = jnp.maximum(first, second)
    return top + log2(jnp.exp2(first - top) + jnp.exp2(second - top))


def kernel(
    n_dp, group,
    scale_ref, v_hbm, t_hbm,
    image_loss, text_loss, image_grad, text_grad,
    rows_buf, scores, acc, peak, total, own_col, got_col, own_row, got_row, lanes, column, losses, diagonal,
    send_sem, recv_sem, col_send, col_recv, row_send, row_recv, lane_send, lane_recv, load_sem, out_sem,
):
    half, width = v_hbm.shape
    chunk = half // CHUNKS
    part_rows = half // 2
    per_part = CHUNKS // 2
    b = lax.axis_index("dp")
    h = lax.axis_index("dup")
    odd = b % 2
    place = b % group
    flip_t = jnp.where(place >= group - 2, 1, 0)
    flip_v = jnp.where(place < 2, 1, 0)

    def block(by):
        return (b + by + n_dp) % n_dp

    other = (b, 1 - h)
    mate = (b + 1 - 2 * odd, h)
    down = (block(-2), (h + flip_v) % 2)
    up = (block(2), (h + flip_t) % 2)

    load_t = pltpu.make_async_copy(t_hbm, rows_buf.at[0], load_sem.at[0])
    load_v = pltpu.make_async_copy(v_hbm, rows_buf.at[6], load_sem.at[1])
    load_t.start()
    load_v.start()

    barrier = pltpu.get_barrier_semaphore()
    peers = [other] + [(block(by), q) for by in (-2, -1, 1, 2) for q in (0, 1)]
    for peer in peers:
        pl.semaphore_signal(barrier, inc=1, device_id=peer, device_id_type=MESH)
    pl.semaphore_wait(barrier, len(peers))

    scale = scale_ref[0]
    scale2 = scale * LOG2E

    def copy(slot, k):
        where = slot % 6
        is_v = slot // 6
        if where == 1:
            source, peer = slot - 1, other
        elif where == 4:
            source, peer = slot - 4, (up if is_v else down)
        elif where == 5:
            source, peer = slot - 4, (up if is_v else down)
        else:
            ahead = odd if is_v else 1 - odd
            source, peer = 6 * is_v + (where - 2) + 4 * ahead, mate
        at = pl.ds(pl.multiple_of(k * chunk, chunk), chunk)
        return pltpu.make_async_remote_copy(
            rows_buf.at[source, at], rows_buf.at[slot, at],
            send_sem.at[slot, k], recv_sem.at[slot, k], device_id=peer, device_id_type=MESH,
        )

    def send_all(slot, first=0):
        @pl.loop(first, CHUNKS)
        def _(k):
            copy(slot, k).start()

    def arrived(slot, k):
        at = pl.ds(pl.multiple_of(k * chunk, chunk), chunk)
        pltpu.make_async_remote_copy(
            rows_buf.at[slot, at], rows_buf.at[slot, at],
            send_sem.at[1, 0], recv_sem.at[slot, k], device_id=other, device_id_type=MESH,
        ).wait_recv()

    def part_arrived(slot, part):
        @pl.loop(0, per_part)
        def _(k):
            arrived(slot, part * per_part + k)

    load_t.wait()
    send_all(1)

    @pl.when(odd == 0)
    def _():
        send_all(4)

    load_v.wait()

    @pl.when(odd == 1)
    def _():
        send_all(10)
        send_all(2)

    @pl.when(odd == 0)
    def _():
        send_all(8)

    peak[...] = jnp.full(peak.shape, LOW, jnp.float32)
    total[...] = jnp.zeros(total.shape, jnp.float32)
    acc[...] = jnp.zeros(acc.shape, jnp.float32)

    def first_events(k):
        arrived(1, k)

        @pl.when(odd == 0)
        def _():
            copy(5, k).start()

            @pl.when(k < per_part)
            def _():
                for j in range(2):
                    arrived(4, 2 * k + j)
                    copy(2, 2 * k + j).start()

            @pl.when(k >= per_part)
            def _():
                for j in range(2):
                    arrived(5, 2 * (k - per_part) + j)
                    copy(3, 2 * (k - per_part) + j).start()

            @pl.when(k == per_part)
            def _():
                send_all(10)

        @pl.when(odd == 1)
        def _():
            copy(3, k).start()

            @pl.when(k < per_part)
            def _():
                for j in range(2):
                    arrived(10, 2 * k + j)
                    copy(8, 2 * k + j).start()

        @pl.when(k == CHUNKS - 2)
        def _():
            copy(7, 0).start()

        @pl.when(k == CHUNKS - 1)
        def _():
            send_all(7, 1)

            @pl.when(odd == 1)
            def _():
                send_all(4)
                send_all(5)

    def half_of(part):
        return pl.ds(pl.multiple_of(part * part_rows, part_rows), part_rows)

    def product(left, slot, part):
        return (
            lax.dot_general(
                rows_buf[left], rows_buf[slot, half_of(part)], (((1,), (1,)), ((), ())),
                preferred_element_type=jnp.float32,
            )
            * scale2
        )

    @pl.loop(0, len(FIRST_EVEN))
    def _(n):
        upto, slot, part = looked_up(n, odd, FIRST_EVEN, FIRST_ODD)
        since, _, _ = looked_up(jnp.maximum(n - 1, 0), odd, FIRST_EVEN, FIRST_ODD)

        @pl.loop(since, upto)
        def _(k):
            first_events(k)

        @pl.when((slot == 2) | (slot == 3))
        def _():
            part_arrived(slot, part)

        far = jnp.where((odd == 1) & (slot >= 4), 1, 0)
        tile = product(6 + 4 * far, slot - 4 * far, part)
        scores[slot, :, half_of(part)] = tile
        before = peak[far]
        now = jnp.maximum(before, tile.max(axis=1, keepdims=True))
        peak[far] = now
        summed = jnp.exp2(tile - wide(now, part_rows)).sum(axis=1, keepdims=True)
        total[far] = total[far] * jnp.exp2(before - now) + summed
        top = tile.max(axis=0, keepdims=True)
        own_col[slot, :, half_of(part)] = top + log2(jnp.exp2(tile - top).sum(axis=0, keepdims=True))

        early = jnp.where(odd == 1, n < 6, (n < 2) | ((n >= 7) & (n < 9)))

        @pl.when(early)
        def _():
            even_slot = jnp.where(n < 2, 6, 8)
            even_part = jnp.where(n < 2, n, n - 7)
            e_slot = jnp.where(odd == 1, 6 + 2 * (n // 2), even_slot)
            e_part = jnp.where(odd == 1, n % 2, even_part)

            @pl.when(e_slot == 8)
            def _():
                part_arrived(8, e_part)

            scores[e_slot, :, half_of(e_part)] = product(0, e_slot, e_part)

    label_next = (h + odd * flip_t) % 2
    label_after = (h + flip_t) % 2

    def small(source, target, sends, recvs, at, peer):
        return pltpu.make_async_remote_copy(
            source, target, sends, recvs.at[at], device_id=peer, device_id_type=MESH
        )

    @pl.when(odd == 1)
    def _():
        for slot in range(2):
            own_col[slot] = merged(own_col[slot], own_col[slot + 4])

    col_to = small(own_col.at[1], got_col.at[1], col_send.at[1], col_recv, 1, other)
    col_next = [
        small(own_col.at[2 + j], got_col.at[2 + h], col_send.at[2 + j], col_recv, 2 + h, (block(1), (label_next + j) % 2))
        for j in range(2)
    ]
    col_after = [
        small(own_col.at[4 + j], got_col.at[4 + h], col_send.at[4 + j], col_recv, 4 + h, (block(2), (label_after + j) % 2))
        for j in range(2)
    ]
    row_back = small(own_row.at[1], got_row.at[0], row_send.at[0], row_recv, 0, down)
    for each in [*col_next, col_to]:
        each.start()

    @pl.when(odd == 0)
    def _():
        for each in col_after:
            each.start()

    @pl.when(odd == 1)
    def _():
        own_row[1] = jnp.transpose(peak[1] + log2(total[1]))[:1]
        row_back.start()
        for slot in (4, 5):
            got_col[slot] = jnp.full(got_col.shape[1:], LOW, jnp.float32)

    own_row[0] = jnp.transpose(peak[0] + log2(total[0]))[:1]
    same = lax.broadcasted_iota(jnp.int32, (half, half), 0) == lax.broadcasted_iota(jnp.int32, (half, half), 1)
    diagonal[...] = jnp.where(same, scores[0], 0.0).sum(axis=0, keepdims=True)

    @pl.when(odd == 0)
    def _():
        lanes[6] = own_row[0]

    @pl.when(odd == 1)
    def _():
        row_back.wait_recv()
        lanes[6] = merged(own_row[0], got_row[0])

    row_to = [small(lanes.at[6], lanes.at[7], lane_send.at[6], lane_recv, 7, other)]
    row_to += [
        small(lanes.at[6], lanes.at[6 + 2 * by + h], lane_send.at[5 + 2 * by + q], lane_recv, 6 + 2 * by + h, (block(by), q))
        for by in (1, 2) for q in (0, 1)
    ]
    for each in row_to:
        each.start()

    def col_arrived(at):
        small(own_col.at[1], got_col.at[at], col_send.at[1], col_recv, at, other).wait_recv()

    for at in (1, 2, 3):
        col_arrived(at)

    @pl.when(odd == 0)
    def _():
        for at in (4, 5):
            col_arrived(at)

    terms = [own_col[0]] + [got_col[at] for at in range(1, 6)]
    top = functools.reduce(jnp.maximum, terms)
    lanes[0] = top + log2(functools.reduce(jnp.add, [jnp.exp2(term - top) for term in terms]))
    col_back = [small(lanes.at[0], lanes.at[1], lane_send.at[0], lane_recv, 1, other)]
    col_back += [
        small(lanes.at[0], lanes.at[2 * by + h], lane_send.at[2 * by - 1 + q], lane_recv, 2 * by + h, (block(-by), q))
        for by in (1, 2) for q in (0, 1)
    ]
    for each in col_back:
        each.start()

    def spread(row):
        return jnp.transpose(jnp.broadcast_to(row, (128, half)))

    column[0] = spread(lanes[6])
    column[1] = spread(lanes[0])
    losses[0] = LN2 * (lanes[6] - diagonal[...])
    losses[1] = LN2 * (lanes[0] - diagonal[...])
    loss_out = [
        pltpu.make_async_copy(losses.at[i], ref, out_sem.at[i]) for i, ref in enumerate((image_loss, text_loss))
    ]
    for each in loss_out:
        each.start()

    @pl.loop(1, 6)
    def _(at):
        for base in (0, 6):
            small(lanes.at[0], lanes.at[base + at], lane_send.at[0], lane_recv, base + at, other).wait_recv()

    def second_events(k):
        @pl.when(k < CHUNKS)
        def _():
            arrived(7, k)
            copy(11, k).start()

            @pl.when(odd == 0)
            def _():
                copy(9, k).start()

        @pl.when((k > 0) & (odd == 1))
        def _():
            arrived(11, k - 1)
            copy(9, k - 1).start()

    def lane_of(slot):
        where = slot % 6
        side = slot // 6
        flipped = jnp.where(side == 0, flip_t, flip_v)
        straight = (where < 4) & (odd == side)
        label = (h + jnp.where(straight, 0, flipped) + where % 2) % 2
        return jnp.where(where < 2, slot, slot - where % 2 + label)

    def finish(side, own, ref):
        @pl.loop(0, CHUNKS)
        def _(k):
            at = pl.ds(pl.multiple_of(k * chunk, chunk), chunk)
            acc[side, at] = scale * acc[side, at] - 2.0 * scale * rows_buf[own, at].astype(jnp.float32)

        pltpu.make_async_copy(acc.at[side], ref, out_sem.at[2 + side]).start()

    steps = len(SECOND_EVEN)

    @pl.loop(0, steps)
    def _(n):
        upto, slot, part = looked_up(n, odd, SECOND_EVEN, SECOND_ODD)
        since, _, _ = looked_up(jnp.maximum(n - 1, 0), odd, SECOND_EVEN, SECOND_ODD)
        since = jnp.where(n == 0, 0, since)

        @pl.loop(since, upto)
        def _(k):
            second_events(k)

        side = slot // 6
        late = jnp.where(odd == 1, (slot == 4) | (slot == 5), (slot == 10) | (slot == 11))

        @pl.when(late | (slot == 9))
        def _():
            part_arrived(slot, part)

        @pl.when(late | (slot == 7) | (slot == 9) | (slot == 11))
        def _():
            scores[slot, :, half_of(part)] = product(6 * (1 - side), slot, part)

        tile = scores[slot, :, half_of(part)]
        weights = (
            jnp.exp2(tile - wide(column[side], part_rows)) + jnp.exp2(tile - lanes[lane_of(slot), :, half_of(part)])
        ).astype(jnp.bfloat16)
        for at in range(0, width, 256):
            cols = pl.ds(at, min(256, width))
            acc[side, :, cols] += jnp.dot(
                weights, rows_buf[slot, half_of(part), cols], preferred_element_type=jnp.float32
            )

        @pl.when(n == jnp.where(odd == 1, steps - 1, 11))
        def _():
            finish(0, 0, image_grad)

    finish(1, 6, text_grad)

    @pl.loop(0, CHUNKS)
    def _(k):
        for slot in (1, 2, 3, 4, 5, 7, 8, 9, 10, 11):
            copy(slot, k).wait_send()

    for each in [*col_next, col_to, *row_to, *col_back]:
        each.wait_send()

    @pl.when(odd == 0)
    def _():
        for each in col_after:
            each.wait_send()

    @pl.when(odd == 1)
    def _():
        row_back.wait_send()

    for each in loss_out:
        each.wait()
    for side, ref in enumerate((image_grad, text_grad)):
        pltpu.make_async_copy(acc.at[side], ref, out_sem.at[2 + side]).wait()


def shards(n_dp, group, v, t, scale):
    half, width = v.shape
    f32, bf16 = jnp.float32, jnp.bfloat16
    dma = pltpu.SemaphoreType.DMA
    row = jax.ShapeDtypeStruct((1, half), f32)
    grad = jax.ShapeDtypeStruct((half, width), f32)
    anywhere = pl.BlockSpec(memory_space=pl.ANY)
    image_loss, text_loss, image_grad, text_grad = pl.pallas_call(
        functools.partial(kernel, n_dp, group),
        out_shape=(row, row, grad, grad),
        in_specs=[pl.BlockSpec(memory_space=pltpu.SMEM), anywhere, anywhere],
        out_specs=(anywhere,) * 4,
        scratch_shapes=[
            pltpu.VMEM((12, half, width), bf16),
            pltpu.VMEM((12, half, half), f32),
            pltpu.VMEM((2, half, width), f32),
            pltpu.VMEM((2, half, 128), f32),
            pltpu.VMEM((2, half, 128), f32),
            pltpu.VMEM((6, 1, half), f32),
            pltpu.VMEM((6, 1, half), f32),
            pltpu.VMEM((2, 1, half), f32),
            pltpu.VMEM((1, 1, half), f32),
            pltpu.VMEM((12, 1, half), f32),
            pltpu.VMEM((2, half, 128), f32),
            pltpu.VMEM((2, 1, half), f32),
            pltpu.VMEM((1, half), f32),
            dma((12, CHUNKS)),
            dma((12, CHUNKS)),
            dma((6,)),
            dma((6,)),
            dma((1,)),
            dma((1,)),
            dma((12,)),
            dma((12,)),
            dma((2,)),
            dma((4,)),
        ],
        compiler_params=pltpu.CompilerParams(
            collective_id=0, has_side_effects=True, vmem_limit_bytes=60 << 20
        ),
        cost_estimate=pl.CostEstimate(flops=13_000_000_000, bytes_accessed=6 << 20, transcendentals=10_000_000),
    )(scale, v, t)
    return image_loss.reshape(half), text_loss.reshape(half), image_grad, text_grad


def solution(mesh):
    n_dp = mesh.shape["dp"]
    split = P(("dp", "dup"), None)
    flat = P(("dp", "dup"))
    return jax.shard_map(
        functools.partial(shards, n_dp, n_dp // 2),
        mesh=mesh,
        in_specs=(split, split, P()),
        out_specs=(flat, flat, split, split),
        check_vma=False,
    )
```

```python
import functools
import math

import jax
import jax.numpy as jnp
from jax import lax
from jax.experimental import pallas as pl
from jax.experimental.pallas import tpu as pltpu
from jax.sharding import PartitionSpec as P

MESH = pl.DeviceIdType.MESH
LOG2E = math.log2(math.e)
LN2 = math.log(2.0)
CHUNKS = 8
LOW = -1e30

FIRST_EVEN = [
    (0, 0, 0), (0, 0, 1), (1, 2, 0), (2, 2, 1), (4, 1, 0), (4, 4, 0),
    (5, 4, 1), (6, 3, 0), (7, 5, 0), (8, 1, 1), (8, 3, 1), (8, 5, 1),
]
FIRST_ODD = [
    (0, 0, 0), (0, 0, 1), (4, 1, 0), (4, 2, 0), (5, 4, 0), (5, 4, 1),
    (6, 5, 0), (7, 2, 1), (7, 3, 0), (8, 1, 1), (8, 5, 1), (8, 3, 1),
]
SECOND_EVEN = [
    (3, 0, 0), (3, 0, 1), (4, 1, 0), (4, 1, 1), (4, 2, 0), (4, 2, 1),
    (4, 3, 0), (5, 3, 1), (5, 4, 0), (5, 4, 1), (5, 5, 0), (5, 5, 1),
    (6, 6, 0), (6, 6, 1), (6, 8, 0), (6, 8, 1), (6, 10, 0), (7, 10, 1),
    (7, 7, 0), (7, 11, 0), (7, 9, 0), (8, 7, 1), (9, 11, 1), (9, 9, 1),
]
SECOND_ODD = [
    (3, 0, 0), (3, 0, 1), (4, 1, 0), (4, 1, 1), (4, 2, 0), (4, 2, 1),
    (4, 3, 0), (5, 3, 1), (5, 6, 0), (5, 6, 1), (5, 8, 0), (5, 8, 1),
    (6, 10, 0), (6, 10, 1), (6, 4, 0), (6, 4, 1), (6, 7, 0), (7, 11, 0),
    (7, 9, 0), (7, 5, 0), (8, 7, 1), (9, 5, 1), (9, 11, 1), (9, 9, 1),
]


def looked_up(index, odd, even_list, odd_list):
    def words(entries):
        codes = [k * 32 + slot * 2 + part for k, slot, part in entries]
        codes += [0] * (-len(codes) % 3)
        return [sum(c << (9 * i) for i, c in enumerate(codes[at : at + 3])) for at in range(0, len(codes), 3)]

    group = index // 3
    word = jnp.int32(0)
    for at, (even_word, odd_word) in enumerate(zip(words(even_list), words(odd_list))):
        word = jnp.where(group == at, jnp.where(odd == 1, odd_word, even_word), word)
    code = lax.shift_right_logical(word, 9 * (index - group * 3)) & 511
    return code // 32, (code % 32) // 2, code % 2


def wide(column, count):
    return jnp.concatenate([column] * (count // 128), axis=1)


def log2(value):
    return jnp.log(value) * LOG2E


def merged(first, second):
    top = jnp.maximum(first, second)
    return top + log2(jnp.exp2(first - top) + jnp.exp2(second - top))


def kernel(
    n_dp, group,
    scale_ref, v_hbm, t_hbm,
    image_loss, text_loss, image_grad, text_grad,
    rows_buf, scores, acc, peak, total, own_col, got_col, own_row, got_row, lanes, column, diagonal,
    send_sem, recv_sem, col_send, col_recv, row_send, row_recv, lane_send, lane_recv, load_sem,
):
    half, width = v_hbm.shape
    chunk = half // CHUNKS
    part_rows = half // 2
    per_part = CHUNKS // 2
    b = lax.axis_index("dp")
    h = lax.axis_index("dup")
    odd = b % 2
    place = b % group
    flip_t = jnp.where(place >= group - 2, 1, 0)
    flip_v = jnp.where(place < 2, 1, 0)

    def block(by):
        return (b + by + n_dp) % n_dp

    other = (b, 1 - h)
    mate = (b + 1 - 2 * odd, h)
    down = (block(-2), (h + flip_v) % 2)
    up = (block(2), (h + flip_t) % 2)

    load_t = pltpu.make_async_copy(t_hbm, rows_buf.at[0], load_sem.at[0])
    load_v = pltpu.make_async_copy(v_hbm, rows_buf.at[6], load_sem.at[1])
    load_t.start()
    load_v.start()

    barrier = pltpu.get_barrier_semaphore()
    peers = [other] + [(block(by), q) for by in (-2, -1, 1, 2) for q in (0, 1)]
    for peer in peers:
        pl.semaphore_signal(barrier, inc=1, device_id=peer, device_id_type=MESH)
    pl.semaphore_wait(barrier, len(peers))

    scale = scale_ref[0]
    scale2 = scale * LOG2E

    def copy(slot, k):
        where = slot % 6
        is_v = slot // 6
        if where == 1:
            source, peer = slot - 1, other
        elif where == 4:
            source, peer = slot - 4, (up if is_v else down)
        elif where == 5:
            source, peer = slot - 4, (up if is_v else down)
        else:
            ahead = odd if is_v else 1 - odd
            source, peer = 6 * is_v + (where - 2) + 4 * ahead, mate
        at = pl.ds(pl.multiple_of(k * chunk, chunk), chunk)
        return pltpu.make_async_remote_copy(
            rows_buf.at[source, at], rows_buf.at[slot, at],
            send_sem.at[slot, k], recv_sem.at[slot, k], device_id=peer, device_id_type=MESH,
        )

    def send_all(slot, first=0, last=CHUNKS):
        @pl.loop(first, last)
        def _(k):
            copy(slot, k).start()

    def arrived(slot, k):
        at = pl.ds(pl.multiple_of(k * chunk, chunk), chunk)
        pltpu.make_async_remote_copy(
            rows_buf.at[slot, at], rows_buf.at[slot, at],
            send_sem.at[1, 0], recv_sem.at[slot, k], device_id=other, device_id_type=MESH,
        ).wait_recv()

    def part_arrived(slot, part):
        @pl.loop(0, per_part)
        def _(k):
            arrived(slot, part * per_part + k)

    load_t.wait()
    send_all(1)

    @pl.when(odd == 0)
    def _():
        send_all(4)

    load_v.wait()

    @pl.when(odd == 1)
    def _():
        send_all(10)
        send_all(2)

    @pl.when(odd == 0)
    def _():
        send_all(8)

    peak[...] = jnp.full(peak.shape, LOW, jnp.float32)
    total[...] = jnp.zeros(total.shape, jnp.float32)
    acc[...] = jnp.zeros(acc.shape, jnp.float32)

    def first_events(k):
        arrived(1, k)

        @pl.when(odd == 0)
        def _():
            copy(5, k).start()

            @pl.when(k < per_part)
            def _():
                for j in range(2):
                    arrived(4, 2 * k + j)
                    copy(2, 2 * k + j).start()

            @pl.when(k >= per_part)
            def _():
                for j in range(2):
                    arrived(5, 2 * (k - per_part) + j)
                    copy(3, 2 * (k - per_part) + j).start()

            @pl.when(k == per_part)
            def _():
                send_all(10)

        @pl.when(odd == 1)
        def _():
            copy(3, k).start()

            @pl.when(k < per_part)
            def _():
                for j in range(2):
                    arrived(10, 2 * k + j)
                    copy(8, 2 * k + j).start()

        @pl.when(k == CHUNKS - 2)
        def _():
            copy(7, 0).start()

        @pl.when(k == CHUNKS - 1)
        def _():
            copy(7, 1).start()

            @pl.when(odd == 1)
            def _():
                send_all(4, 0, 2)

    def half_of(part):
        return pl.ds(pl.multiple_of(part * part_rows, part_rows), part_rows)

    def product(left, slot, part):
        return (
            lax.dot_general(
                rows_buf[left], rows_buf[slot, half_of(part)], (((1,), (1,)), ((), ())),
                preferred_element_type=jnp.float32,
            )
            * scale2
        )

    @pl.loop(0, len(FIRST_EVEN))
    def _(n):
        upto, slot, part = looked_up(n, odd, FIRST_EVEN, FIRST_ODD)
        since, _, _ = looked_up(jnp.maximum(n - 1, 0), odd, FIRST_EVEN, FIRST_ODD)

        @pl.loop(since, upto)
        def _(k):
            first_events(k)

        @pl.when((slot == 2) | (slot == 3))
        def _():
            part_arrived(slot, part)

        far = jnp.where((odd == 1) & (slot >= 4), 1, 0)
        tile = product(6 + 4 * far, slot - 4 * far, part)
        scores[slot, :, half_of(part)] = tile
        before = peak[far]
        now = jnp.maximum(before, tile.max(axis=1, keepdims=True))
        peak[far] = now
        summed = jnp.exp2(tile - wide(now, part_rows)).sum(axis=1, keepdims=True)
        total[far] = total[far] * jnp.exp2(before - now) + summed
        top = tile.max(axis=0, keepdims=True)
        own_col[slot, :, half_of(part)] = top + log2(jnp.exp2(tile - top).sum(axis=0, keepdims=True))

        early = jnp.where(odd == 1, n < 6, (n < 2) | ((n >= 7) & (n < 9)))

        @pl.when(early)
        def _():
            even_slot = jnp.where(n < 2, 6, 8)
            even_part = jnp.where(n < 2, n, n - 7)
            e_slot = jnp.where(odd == 1, 6 + 2 * (n // 2), even_slot)
            e_part = jnp.where(odd == 1, n % 2, even_part)

            @pl.when(e_slot == 8)
            def _():
                part_arrived(8, e_part)

            scores[e_slot, :, half_of(e_part)] = product(0, e_slot, e_part)

    def second_events(k):
        @pl.when(k < CHUNKS)
        def _():
            arrived(7, k)
            copy(11, k).start()

            @pl.when(odd == 0)
            def _():
                copy(9, k).start()

        @pl.when((k > 0) & (odd == 1))
        def _():
            arrived(11, k - 1)
            copy(9, k - 1).start()

    label_next = (h + odd * flip_t) % 2
    label_after = (h + flip_t) % 2

    def small(source, target, sends, recvs, at, peer):
        return pltpu.make_async_remote_copy(
            source, target, sends, recvs.at[at], device_id=peer, device_id_type=MESH
        )

    @pl.when(odd == 1)
    def _():
        for slot in range(2):
            own_col[slot] = merged(own_col[slot], own_col[slot + 4])

    col_to = small(own_col.at[1], got_col.at[1], col_send.at[1], col_recv, 1, other)
    col_next = [
        small(own_col.at[2 + j], got_col.at[2 + h], col_send.at[2 + j], col_recv, 2 + h, (block(1), (label_next + j) % 2))
        for j in range(2)
    ]
    col_after = [
        small(own_col.at[4 + j], got_col.at[4 + h], col_send.at[4 + j], col_recv, 4 + h, (block(2), (label_after + j) % 2))
        for j in range(2)
    ]
    row_back = small(own_row.at[1], got_row.at[0], row_send.at[0], row_recv, 0, down)
    for each in [*col_next, col_to]:
        each.start()

    @pl.when(odd == 0)
    def _():
        for each in col_after:
            each.start()

    @pl.when(odd == 1)
    def _():
        own_row[1] = jnp.transpose(peak[1] + log2(total[1]))[:1]
        row_back.start()
        for slot in (4, 5):
            got_col[slot] = jnp.full(got_col.shape[1:], LOW, jnp.float32)

    send_all(7, 2, 4)

    @pl.when(odd == 1)
    def _():
        send_all(4, 2, 6)

    own_row[0] = jnp.transpose(peak[0] + log2(total[0]))[:1]
    same = lax.broadcasted_iota(jnp.int32, (half, half), 0) == lax.broadcasted_iota(jnp.int32, (half, half), 1)
    diagonal[...] = jnp.where(same, scores[0], 0.0).sum(axis=0, keepdims=True)

    @pl.when(odd == 0)
    def _():
        lanes[6] = own_row[0]

    @pl.when(odd == 1)
    def _():
        row_back.wait_recv()
        lanes[6] = merged(own_row[0], got_row[0])

    row_to = [small(lanes.at[6], lanes.at[7], lane_send.at[6], lane_recv, 7, other)]
    row_to += [
        small(lanes.at[6], lanes.at[6 + 2 * by + h], lane_send.at[5 + 2 * by + q], lane_recv, 6 + 2 * by + h, (block(by), q))
        for by in (1, 2) for q in (0, 1)
    ]
    second_events(0)

    def col_arrived(at):
        small(own_col.at[1], got_col.at[at], col_send.at[1], col_recv, at, other).wait_recv()

    for at in (1, 2, 3):
        col_arrived(at)

    @pl.when(odd == 0)
    def _():
        for at in (4, 5):
            col_arrived(at)

    terms = [own_col[0]] + [got_col[at] for at in range(1, 6)]
    top = functools.reduce(jnp.maximum, terms)
    lanes[0] = top + log2(functools.reduce(jnp.add, [jnp.exp2(term - top) for term in terms]))
    col_back = [small(lanes.at[0], lanes.at[1], lane_send.at[0], lane_recv, 1, other)]
    col_back += [
        small(lanes.at[0], lanes.at[2 * by + h], lane_send.at[2 * by - 1 + q], lane_recv, 2 * by + h, (block(-by), q))
        for by in (1, 2) for q in (0, 1)
    ]
    for each in [*col_back, *row_to]:
        each.start()

    send_all(7, 4)

    @pl.when(odd == 1)
    def _():
        send_all(4, 6)
        send_all(5)

    second_events(1)

    def spread(row):
        return jnp.transpose(jnp.broadcast_to(row, (128, half)))

    column[0] = spread(lanes[6])
    column[1] = spread(lanes[0])
    image_loss[...] = LN2 * (lanes[6] - diagonal[...])
    text_loss[...] = LN2 * (lanes[0] - diagonal[...])
    @pl.when(odd == 0)
    def _():
        for part in range(2):
            part_arrived(10, part)
            scores[10, :, half_of(part)] = product(0, 10, part)

    @pl.loop(1, 6)
    def _(at):
        for base in (0, 6):
            small(lanes.at[0], lanes.at[base + at], lane_send.at[0], lane_recv, base + at, other).wait_recv()

    def lane_of(slot):
        where = slot % 6
        side = slot // 6
        flipped = jnp.where(side == 0, flip_t, flip_v)
        straight = (where < 4) & (odd == side)
        label = (h + jnp.where(straight, 0, flipped) + where % 2) % 2
        return jnp.where(where < 2, slot, slot - where % 2 + label)

    def finish(side, own, ref):
        @pl.loop(0, CHUNKS)
        def _(k):
            at = pl.ds(pl.multiple_of(k * chunk, chunk), chunk)
            ref[at] = scale * acc[side, at] - 2.0 * scale * rows_buf[own, at].astype(jnp.float32)


    steps = len(SECOND_EVEN)

    @pl.loop(0, steps)
    def _(n):
        upto, slot, part = looked_up(n, odd, SECOND_EVEN, SECOND_ODD)
        since, _, _ = looked_up(jnp.maximum(n - 1, 0), odd, SECOND_EVEN, SECOND_ODD)
        since = jnp.where(n == 0, 2, since)

        @pl.loop(since, upto)
        def _(k):
            second_events(k)

        side = slot // 6
        late = jnp.where(odd == 1, (slot == 4) | (slot == 5), slot == 11)

        @pl.when(late | (slot == 9))
        def _():
            part_arrived(slot, part)

        @pl.when(late | (slot == 7) | (slot == 9) | (slot == 11))
        def _():
            scores[slot, :, half_of(part)] = product(6 * (1 - side), slot, part)

        tile = scores[slot, :, half_of(part)]
        weights = (
            jnp.exp2(tile - wide(column[side], part_rows)) + jnp.exp2(tile - lanes[lane_of(slot), :, half_of(part)])
        ).astype(jnp.bfloat16)
        for at in range(0, width, 256):
            cols = pl.ds(at, min(256, width))
            acc[side, :, cols] += jnp.dot(
                weights, rows_buf[slot, half_of(part), cols], preferred_element_type=jnp.float32
            )

        @pl.when(n == jnp.where(odd == 1, steps - 1, 11))
        def _():
            finish(0, 0, image_grad)

    finish(1, 6, text_grad)

    @pl.loop(0, CHUNKS)
    def _(k):
        for slot in (1, 2, 3, 4, 5, 7, 8, 9, 10, 11):
            copy(slot, k).wait_send()

    for each in [*col_next, col_to, *row_to, *col_back]:
        each.wait_send()

    @pl.when(odd == 0)
    def _():
        for each in col_after:
            each.wait_send()

    @pl.when(odd == 1)
    def _():
        row_back.wait_send()


def placed(*refs):
    half = len(refs) // 2
    sources, targets, sem = refs[:half], refs[half : 2 * half], refs[2 * half]
    copies = [pltpu.make_async_copy(a, b, sem.at[i]) for i, (a, b) in enumerate(zip(sources, targets))]
    for each in copies:
        each.start()
    for each in copies:
        each.wait()


def shards(n_dp, group, v, t, scale):
    half, width = v.shape
    f32, bf16 = jnp.float32, jnp.bfloat16
    dma = pltpu.SemaphoreType.DMA
    row = jax.ShapeDtypeStruct((1, half), f32)
    grad = jax.ShapeDtypeStruct((half, width), f32)
    near = pl.BlockSpec(memory_space=pltpu.VMEM)
    far = pl.BlockSpec(memory_space=pltpu.HBM)
    results = pl.pallas_call(
        functools.partial(kernel, n_dp, group),
        out_shape=(row, row, grad, grad),
        in_specs=[pl.BlockSpec(memory_space=pltpu.SMEM), far, far],
        out_specs=(near,) * 4,
        scratch_shapes=[
            pltpu.VMEM((12, half, width), bf16),
            pltpu.VMEM((12, half, half), f32),
            pltpu.VMEM((2, half, width), f32),
            pltpu.VMEM((2, half, 128), f32),
            pltpu.VMEM((2, half, 128), f32),
            pltpu.VMEM((6, 1, half), f32),
            pltpu.VMEM((6, 1, half), f32),
            pltpu.VMEM((2, 1, half), f32),
            pltpu.VMEM((1, 1, half), f32),
            pltpu.VMEM((12, 1, half), f32),
            pltpu.VMEM((2, half, 128), f32),
            pltpu.VMEM((1, half), f32),
            dma((12, CHUNKS)),
            dma((12, CHUNKS)),
            dma((6,)),
            dma((6,)),
            dma((1,)),
            dma((1,)),
            dma((12,)),
            dma((12,)),
            dma((2,)),
        ],
        compiler_params=pltpu.CompilerParams(
            collective_id=0, has_side_effects=True, vmem_limit_bytes=44 << 20
        ),
        cost_estimate=pl.CostEstimate(flops=13_000_000_000, bytes_accessed=6 << 20, transcendentals=10_000_000),
    )(scale, v, t)
    image_loss, text_loss, image_grad, text_grad = pl.pallas_call(
        placed,
        out_shape=(row, row, grad, grad),
        in_specs=[near] * 4,
        out_specs=(far,) * 4,
        scratch_shapes=[dma((4,))],
        compiler_params=pltpu.CompilerParams(vmem_limit_bytes=8 << 20),
    )(*results)
    return image_loss.reshape(half), text_loss.reshape(half), image_grad, text_grad


def solution(mesh):
    n_dp = mesh.shape["dp"]
    split = P(("dp", "dup"), None)
    flat = P(("dp", "dup"))
    return jax.shard_map(
        functools.partial(shards, n_dp, n_dp // 2),
        mesh=mesh,
        in_specs=(split, split, P()),
        out_specs=(flat, flat, split, split),
        check_vma=False,
    )
```

```python
import functools
import math

import jax
import jax.numpy as jnp
from jax import lax
from jax.experimental import pallas as pl
from jax.experimental.pallas import tpu as pltpu
from jax.sharding import PartitionSpec as P

MESH = pl.DeviceIdType.MESH
LOG2E = math.log2(math.e)
LN2 = math.log(2.0)
CHUNKS = 8
LOW = -1e30

FIRST_EVEN = [
    (0, 0, 0), (0, 0, 1), (1, 2, 0), (2, 2, 1), (4, 1, 0), (4, 4, 0),
    (5, 4, 1), (6, 3, 0), (7, 5, 0), (8, 1, 1), (8, 3, 1), (8, 5, 1),
]
FIRST_ODD = [
    (0, 0, 0), (0, 0, 1), (4, 1, 0), (4, 2, 0), (5, 4, 0), (5, 4, 1),
    (6, 5, 0), (7, 2, 1), (7, 3, 0), (8, 1, 1), (8, 5, 1), (8, 3, 1),
]
SECOND_EVEN = [
    (3, 0, 0), (3, 0, 1), (3, 6, 0), (3, 6, 1), (4, 8, 0), (4, 8, 1),
    (4, 10, 0), (4, 10, 1), (5, 1, 0), (5, 1, 1), (5, 2, 0), (5, 2, 1),
    (5, 3, 0), (6, 3, 1), (6, 4, 0), (6, 4, 1), (6, 5, 0), (7, 5, 1),
    (7, 7, 0), (7, 11, 0), (7, 9, 0), (8, 7, 1), (9, 11, 1), (9, 9, 1),
]
SECOND_ODD = [
    (3, 0, 0), (3, 0, 1), (3, 6, 0), (3, 6, 1), (4, 8, 0), (4, 8, 1),
    (4, 10, 0), (4, 10, 1), (5, 1, 0), (5, 1, 1), (5, 2, 0), (5, 2, 1),
    (5, 3, 0), (6, 3, 1), (6, 4, 0), (6, 4, 1), (7, 7, 0), (7, 11, 0),
    (7, 9, 0), (7, 5, 0), (8, 7, 1), (8, 5, 1), (9, 11, 1), (9, 9, 1),
]


def looked_up(index, odd, even_list, odd_list):
    def words(entries):
        codes = [k * 32 + slot * 2 + part for k, slot, part in entries]
        codes += [0] * (-len(codes) % 3)
        return [sum(c << (9 * i) for i, c in enumerate(codes[at : at + 3])) for at in range(0, len(codes), 3)]

    group = index // 3
    word = jnp.int32(0)
    for at, (even_word, odd_word) in enumerate(zip(words(even_list), words(odd_list))):
        word = jnp.where(group == at, jnp.where(odd == 1, odd_word, even_word), word)
    code = lax.shift_right_logical(word, 9 * (index - group * 3)) & 511
    return code // 32, (code % 32) // 2, code % 2


def wide(column, count):
    return jnp.concatenate([column] * (count // 128), axis=1)


def log2(value):
    return jnp.log(value) * LOG2E


def merged(first, second):
    top = jnp.maximum(first, second)
    return top + log2(jnp.exp2(first - top) + jnp.exp2(second - top))


def kernel(
    n_dp, group,
    scale_ref, v_hbm, t_hbm,
    image_loss, text_loss, image_grad, text_grad,
    rows_buf, scores, acc, peak, total, own_col, got_col, own_row, got_row, lanes, column, diagonal,
    send_sem, recv_sem, col_send, col_recv, row_send, row_recv, lane_send, lane_recv, load_sem,
):
    half, width = v_hbm.shape
    chunk = half // CHUNKS
    part_rows = half // 2
    per_part = CHUNKS // 2
    b = lax.axis_index("dp")
    h = lax.axis_index("dup")
    odd = b % 2
    place = b % group
    flip_t = jnp.where(place >= group - 2, 1, 0)
    flip_v = jnp.where(place < 2, 1, 0)

    def block(by):
        return (b + by + n_dp) % n_dp

    other = (b, 1 - h)
    mate = (b + 1 - 2 * odd, h)
    down = (block(-2), (h + flip_v) % 2)
    up = (block(2), (h + flip_t) % 2)

    load_t = pltpu.make_async_copy(t_hbm, rows_buf.at[0], load_sem.at[0])
    load_v = pltpu.make_async_copy(v_hbm, rows_buf.at[6], load_sem.at[1])
    load_t.start()
    load_v.start()

    barrier = pltpu.get_barrier_semaphore()
    peers = [other] + [(block(by), q) for by in (-2, -1, 1, 2) for q in (0, 1)]
    for peer in peers:
        pl.semaphore_signal(barrier, inc=1, device_id=peer, device_id_type=MESH)
    pl.semaphore_wait(barrier, len(peers))

    scale = scale_ref[0]
    scale2 = scale * LOG2E

    def copy(slot, k):
        where = slot % 6
        is_v = slot // 6
        if where == 1:
            source, peer = slot - 1, other
        elif where == 4:
            source, peer = slot - 4, (up if is_v else down)
        elif where == 5:
            source, peer = slot - 4, (up if is_v else down)
        else:
            ahead = odd if is_v else 1 - odd
            source, peer = 6 * is_v + (where - 2) + 4 * ahead, mate
        at = pl.ds(pl.multiple_of(k * chunk, chunk), chunk)
        return pltpu.make_async_remote_copy(
            rows_buf.at[source, at], rows_buf.at[slot, at],
            send_sem.at[slot, k], recv_sem.at[slot, k], device_id=peer, device_id_type=MESH,
        )

    def send_all(slot, first=0, last=CHUNKS):
        @pl.loop(first, last)
        def _(k):
            copy(slot, k).start()

    def arrived(slot, k):
        at = pl.ds(pl.multiple_of(k * chunk, chunk), chunk)
        pltpu.make_async_remote_copy(
            rows_buf.at[slot, at], rows_buf.at[slot, at],
            send_sem.at[1, 0], recv_sem.at[slot, k], device_id=other, device_id_type=MESH,
        ).wait_recv()

    def part_arrived(slot, part):
        @pl.loop(0, per_part)
        def _(k):
            arrived(slot, part * per_part + k)

    load_t.wait()
    send_all(1)

    @pl.when(odd == 0)
    def _():
        send_all(4)

    load_v.wait()

    @pl.when(odd == 1)
    def _():
        send_all(10)
        send_all(2)

    @pl.when(odd == 0)
    def _():
        send_all(8)

    peak[...] = jnp.full(peak.shape, LOW, jnp.float32)
    total[...] = jnp.zeros(total.shape, jnp.float32)
    acc[...] = jnp.zeros(acc.shape, jnp.float32)

    def first_events(k):
        arrived(1, k)

        @pl.when(odd == 0)
        def _():
            copy(5, k).start()

            @pl.when(k < per_part)
            def _():
                for j in range(2):
                    arrived(4, 2 * k + j)
                    copy(2, 2 * k + j).start()

            @pl.when(k >= per_part)
            def _():
                for j in range(2):
                    arrived(5, 2 * (k - per_part) + j)
                    copy(3, 2 * (k - per_part) + j).start()

            @pl.when(k == 2)
            def _():
                send_all(10)

        @pl.when(odd == 1)
        def _():
            copy(3, k).start()

            @pl.when(k < per_part)
            def _():
                for j in range(2):
                    arrived(10, 2 * k + j)
                    copy(8, 2 * k + j).start()

        @pl.when(k == CHUNKS - 2)
        def _():
            copy(7, 0).start()

        @pl.when(k == CHUNKS - 1)
        def _():
            @pl.when(odd == 1)
            def _():
                send_all(4, 0, 2)

    def half_of(part):
        return pl.ds(pl.multiple_of(part * part_rows, part_rows), part_rows)

    def product(left, slot, part):
        return (
            lax.dot_general(
                rows_buf[left], rows_buf[slot, half_of(part)], (((1,), (1,)), ((), ())),
                preferred_element_type=jnp.float32,
            )
            * scale2
        )

    @pl.loop(0, len(FIRST_EVEN))
    def _(n):
        upto, slot, part = looked_up(n, odd, FIRST_EVEN, FIRST_ODD)
        since, _, _ = looked_up(jnp.maximum(n - 1, 0), odd, FIRST_EVEN, FIRST_ODD)

        @pl.loop(since, upto)
        def _(k):
            first_events(k)

        @pl.when((slot == 2) | (slot == 3))
        def _():
            part_arrived(slot, part)

        far = jnp.where((odd == 1) & (slot >= 4), 1, 0)
        tile = product(6 + 4 * far, slot - 4 * far, part)
        scores[slot, :, half_of(part)] = tile
        before = peak[far]
        now = jnp.maximum(before, tile.max(axis=1, keepdims=True))
        peak[far] = now
        summed = jnp.exp2(tile - wide(now, part_rows)).sum(axis=1, keepdims=True)
        total[far] = total[far] * jnp.exp2(before - now) + summed
        top = tile.max(axis=0, keepdims=True)
        own_col[slot, :, half_of(part)] = top + log2(jnp.exp2(tile - top).sum(axis=0, keepdims=True))

        early = jnp.where(odd == 1, n < 6, (n < 2) | ((n >= 7) & (n < 9)))

        @pl.when(early)
        def _():
            even_slot = jnp.where(n < 2, 6, 8)
            even_part = jnp.where(n < 2, n, n - 7)
            e_slot = jnp.where(odd == 1, 6 + 2 * (n // 2), even_slot)
            e_part = jnp.where(odd == 1, n % 2, even_part)

            @pl.when(e_slot == 8)
            def _():
                part_arrived(8, e_part)

            scores[e_slot, :, half_of(e_part)] = product(0, e_slot, e_part)

    def second_events(k):
        @pl.when(k < CHUNKS)
        def _():
            arrived(7, k)
            copy(11, k).start()

            @pl.when(odd == 0)
            def _():
                copy(9, k).start()

        @pl.when((k > 0) & (odd == 1))
        def _():
            arrived(11, k - 1)
            copy(9, k - 1).start()

    label_next = (h + odd * flip_t) % 2
    label_after = (h + flip_t) % 2

    def small(source, target, sends, recvs, at, peer):
        return pltpu.make_async_remote_copy(
            source, target, sends, recvs.at[at], device_id=peer, device_id_type=MESH
        )

    @pl.when(odd == 1)
    def _():
        for slot in range(2):
            own_col[slot] = merged(own_col[slot], own_col[slot + 4])

    col_to = small(own_col.at[1], got_col.at[1], col_send.at[1], col_recv, 1, other)
    col_next = [
        small(own_col.at[2 + j], got_col.at[2 + h], col_send.at[2 + j], col_recv, 2 + h, (block(1), (label_next + j) % 2))
        for j in range(2)
    ]
    col_after = [
        small(own_col.at[4 + j], got_col.at[4 + h], col_send.at[4 + j], col_recv, 4 + h, (block(2), (label_after + j) % 2))
        for j in range(2)
    ]
    row_back = small(own_row.at[1], got_row.at[0], row_send.at[0], row_recv, 0, down)
    for each in [*col_next, col_to]:
        each.start()

    @pl.when(odd == 0)
    def _():
        for each in col_after:
            each.start()

    @pl.when(odd == 1)
    def _():
        own_row[1] = jnp.transpose(peak[1] + log2(total[1]))[:1]
        row_back.start()
        for slot in (4, 5):
            got_col[slot] = jnp.full(got_col.shape[1:], LOW, jnp.float32)

    own_row[0] = jnp.transpose(peak[0] + log2(total[0]))[:1]
    same = lax.broadcasted_iota(jnp.int32, (half, half), 0) == lax.broadcasted_iota(jnp.int32, (half, half), 1)
    diagonal[...] = jnp.where(same, scores[0], 0.0).sum(axis=0, keepdims=True)

    row_to = [small(lanes.at[6], lanes.at[7], lane_send.at[6], lane_recv, 7, other)]
    row_to += [
        small(lanes.at[6], lanes.at[6 + 2 * by + h], lane_send.at[5 + 2 * by + q], lane_recv, 6 + 2 * by + h, (block(by), q))
        for by in (1, 2) for q in (0, 1)
    ]

    @pl.when(odd == 0)
    def _():
        lanes[6] = own_row[0]
        for each in row_to:
            each.start()

    send_all(7, 1, 3)

    @pl.when(odd == 1)
    def _():
        send_all(4, 2, 5)

    second_events(0)

    @pl.when(odd == 1)
    def _():
        row_back.wait_recv()
        lanes[6] = merged(own_row[0], got_row[0])
        for each in row_to:
            each.start()

    def col_arrived(at):
        small(own_col.at[1], got_col.at[at], col_send.at[1], col_recv, at, other).wait_recv()

    for at in (1, 2, 3):
        col_arrived(at)

    @pl.when(odd == 0)
    def _():
        for at in (4, 5):
            col_arrived(at)

    terms = [own_col[0]] + [got_col[at] for at in range(1, 6)]
    top = functools.reduce(jnp.maximum, terms)
    lanes[0] = top + log2(functools.reduce(jnp.add, [jnp.exp2(term - top) for term in terms]))
    col_back = [small(lanes.at[0], lanes.at[1], lane_send.at[0], lane_recv, 1, other)]
    col_back += [
        small(lanes.at[0], lanes.at[2 * by + h], lane_send.at[2 * by - 1 + q], lane_recv, 2 * by + h, (block(-by), q))
        for by in (1, 2) for q in (0, 1)
    ]
    for each in col_back:
        each.start()

    send_all(7, 3)

    @pl.when(odd == 1)
    def _():
        send_all(4, 5)
        send_all(5)

    second_events(1)
    second_events(2)

    def spread(row):
        return jnp.transpose(jnp.broadcast_to(row, (128, half)))

    column[0] = spread(lanes[6])
    column[1] = spread(lanes[0])
    image_loss[...] = LN2 * (lanes[6] - diagonal[...])
    text_loss[...] = LN2 * (lanes[0] - diagonal[...])
    def lane_of(slot):
        where = slot % 6
        side = slot // 6
        flipped = jnp.where(side == 0, flip_t, flip_v)
        straight = (where < 4) & (odd == side)
        label = (h + jnp.where(straight, 0, flipped) + where % 2) % 2
        return jnp.where(where < 2, slot, slot - where % 2 + label)

    def finish(side, own, ref):
        @pl.loop(0, CHUNKS)
        def _(k):
            at = pl.ds(pl.multiple_of(k * chunk, chunk), chunk)
            ref[at] = scale * acc[side, at] - 2.0 * scale * rows_buf[own, at].astype(jnp.float32)


    steps = len(SECOND_EVEN)

    @pl.loop(0, steps)
    def _(n):
        upto, slot, part = looked_up(n, odd, SECOND_EVEN, SECOND_ODD)
        since, _, _ = looked_up(jnp.maximum(n - 1, 0), odd, SECOND_EVEN, SECOND_ODD)
        since = jnp.where(n == 0, 3, since)

        @pl.loop(since, upto)
        def _(k):
            second_events(k)

        side = slot // 6
        late = jnp.where(odd == 1, (slot == 4) | (slot == 5), (slot == 10) | (slot == 11))

        @pl.when(late | (slot == 9))
        def _():
            part_arrived(slot, part)

        @pl.when(late | (slot == 7) | (slot == 9) | (slot == 11))
        def _():
            scores[slot, :, half_of(part)] = product(6 * (1 - side), slot, part)

        lane = lane_of(slot)

        @pl.when((part == 0) & (slot % 6 > 0))
        def _():
            small(lanes.at[0], lanes.at[lane], lane_send.at[0], lane_recv, lane, other).wait_recv()

        tile = scores[slot, :, half_of(part)]
        weights = (
            jnp.exp2(tile - wide(column[side], part_rows)) + jnp.exp2(tile - lanes[lane, :, half_of(part)])
        ).astype(jnp.bfloat16)
        for at in range(0, width, 256):
            cols = pl.ds(at, min(256, width))
            acc[side, :, cols] += jnp.dot(
                weights, rows_buf[slot, half_of(part), cols], preferred_element_type=jnp.float32
            )

        @pl.when(n == jnp.where(odd == 1, 21, 17))
        def _():
            finish(0, 0, image_grad)

    finish(1, 6, text_grad)

    @pl.loop(0, CHUNKS)
    def _(k):
        for slot in (1, 2, 3, 4, 5, 7, 8, 9, 10, 11):
            copy(slot, k).wait_send()

    for each in [*col_next, col_to, *row_to, *col_back]:
        each.wait_send()

    @pl.when(odd == 0)
    def _():
        for each in col_after:
            each.wait_send()

    @pl.when(odd == 1)
    def _():
        row_back.wait_send()


def placed(*refs):
    half = len(refs) // 2
    sources, targets, sem = refs[:half], refs[half : 2 * half], refs[2 * half]
    copies = [pltpu.make_async_copy(a, b, sem.at[i]) for i, (a, b) in enumerate(zip(sources, targets))]
    for each in copies:
        each.start()
    for each in copies:
        each.wait()


def shards(n_dp, group, v, t, scale):
    half, width = v.shape
    f32, bf16 = jnp.float32, jnp.bfloat16
    dma = pltpu.SemaphoreType.DMA
    row = jax.ShapeDtypeStruct((1, half), f32)
    grad = jax.ShapeDtypeStruct((half, width), f32)
    near = pl.BlockSpec(memory_space=pltpu.VMEM)
    far = pl.BlockSpec(memory_space=pltpu.HBM)
    results = pl.pallas_call(
        functools.partial(kernel, n_dp, group),
        out_shape=(row, row, grad, grad),
        in_specs=[pl.BlockSpec(memory_space=pltpu.SMEM), far, far],
        out_specs=(near,) * 4,
        scratch_shapes=[
            pltpu.VMEM((12, half, width), bf16),
            pltpu.VMEM((12, half, half), f32),
            pltpu.VMEM((2, half, width), f32),
            pltpu.VMEM((2, half, 128), f32),
            pltpu.VMEM((2, half, 128), f32),
            pltpu.VMEM((6, 1, half), f32),
            pltpu.VMEM((6, 1, half), f32),
            pltpu.VMEM((2, 1, half), f32),
            pltpu.VMEM((1, 1, half), f32),
            pltpu.VMEM((12, 1, half), f32),
            pltpu.VMEM((2, half, 128), f32),
            pltpu.VMEM((1, half), f32),
            dma((12, CHUNKS)),
            dma((12, CHUNKS)),
            dma((6,)),
            dma((6,)),
            dma((1,)),
            dma((1,)),
            dma((12,)),
            dma((12,)),
            dma((2,)),
        ],
        compiler_params=pltpu.CompilerParams(
            collective_id=0, has_side_effects=True, vmem_limit_bytes=44 << 20
        ),
        cost_estimate=pl.CostEstimate(flops=13_000_000_000, bytes_accessed=6 << 20, transcendentals=10_000_000),
    )(scale, v, t)
    image_loss, text_loss, image_grad, text_grad = pl.pallas_call(
        placed,
        out_shape=(row, row, grad, grad),
        in_specs=[near] * 4,
        out_specs=(far,) * 4,
        scratch_shapes=[dma((4,))],
        compiler_params=pltpu.CompilerParams(vmem_limit_bytes=8 << 20),
    )(*results)
    return image_loss.reshape(half), text_loss.reshape(half), image_grad, text_grad


def solution(mesh):
    n_dp = mesh.shape["dp"]
    split = P(("dp", "dup"), None)
    flat = P(("dp", "dup"))
    return jax.shard_map(
        functools.partial(shards, n_dp, n_dp // 2),
        mesh=mesh,
        in_specs=(split, split, P()),
        out_specs=(flat, flat, split, split),
        check_vma=False,
    )
```

```python
import functools
import math

import jax
import jax.numpy as jnp
from jax import lax
from jax.experimental import pallas as pl
from jax.experimental.pallas import tpu as pltpu
from jax.sharding import PartitionSpec as P

MESH = pl.DeviceIdType.MESH
LOG2E = math.log2(math.e)
LN2 = math.log(2.0)
CHUNKS = 8
LOW = -1e30

FIRST_EVEN = [
    (0, 0, 0), (0, 0, 1), (1, 2, 0), (2, 2, 1), (4, 1, 0), (4, 4, 0),
    (5, 4, 1), (6, 3, 0), (7, 5, 0), (8, 1, 1), (8, 3, 1), (8, 5, 1),
]
FIRST_ODD = [
    (0, 0, 0), (0, 0, 1), (4, 1, 0), (4, 2, 0), (5, 4, 0), (5, 4, 1),
    (6, 5, 0), (7, 2, 1), (7, 3, 0), (8, 1, 1), (8, 5, 1), (8, 3, 1),
]
SECOND_EVEN = [
    (2, 0, 0), (2, 0, 1), (3, 6, 0), (3, 6, 1), (4, 8, 0), (4, 8, 1),
    (4, 10, 0), (4, 10, 1), (5, 1, 0), (5, 1, 1), (5, 2, 0), (5, 2, 1),
    (5, 3, 0), (6, 3, 1), (6, 4, 0), (6, 4, 1), (6, 5, 0), (7, 5, 1),
    (7, 7, 0), (7, 11, 0), (7, 9, 0), (8, 7, 1), (9, 11, 1), (9, 9, 1),
]
SECOND_ODD = [
    (2, 0, 0), (2, 0, 1), (3, 6, 0), (3, 6, 1), (4, 8, 0), (4, 8, 1),
    (4, 10, 0), (4, 10, 1), (5, 1, 0), (5, 1, 1), (5, 2, 0), (5, 2, 1),
    (5, 3, 0), (6, 3, 1), (6, 4, 0), (6, 4, 1), (7, 7, 0), (7, 11, 0),
    (7, 9, 0), (7, 5, 0), (8, 7, 1), (8, 5, 1), (9, 11, 1), (9, 9, 1),
]


def looked_up(index, odd, even_list, odd_list):
    def words(entries):
        codes = [k * 32 + slot * 2 + part for k, slot, part in entries]
        codes += [0] * (-len(codes) % 3)
        return [sum(c << (9 * i) for i, c in enumerate(codes[at : at + 3])) for at in range(0, len(codes), 3)]

    group = index // 3
    word = jnp.int32(0)
    for at, (even_word, odd_word) in enumerate(zip(words(even_list), words(odd_list))):
        word = jnp.where(group == at, jnp.where(odd == 1, odd_word, even_word), word)
    code = lax.shift_right_logical(word, 9 * (index - group * 3)) & 511
    return code // 32, (code % 32) // 2, code % 2


def wide(column, count):
    return jnp.concatenate([column] * (count // 128), axis=1)


def log2(value):
    return jnp.log(value) * LOG2E


def merged(first, second):
    top = jnp.maximum(first, second)
    return top + log2(jnp.exp2(first - top) + jnp.exp2(second - top))


def kernel(
    n_dp, group,
    scale_ref, v_hbm, t_hbm,
    image_loss, text_loss, image_grad, text_grad,
    rows_buf, scores, acc, peak, total, own_col, got_col, own_row, got_row, lanes, column, diagonal,
    send_sem, recv_sem, col_send, col_recv, row_send, row_recv, lane_send, lane_recv, load_sem,
):
    half, width = v_hbm.shape
    chunk = half // CHUNKS
    part_rows = half // 2
    per_part = CHUNKS // 2
    b = lax.axis_index("dp")
    h = lax.axis_index("dup")
    odd = b % 2
    place = b % group
    flip_t = jnp.where(place >= group - 2, 1, 0)
    flip_v = jnp.where(place < 2, 1, 0)

    def block(by):
        return (b + by + n_dp) % n_dp

    other = (b, 1 - h)
    mate = (b + 1 - 2 * odd, h)
    down = (block(-2), (h + flip_v) % 2)
    up = (block(2), (h + flip_t) % 2)

    load_t = pltpu.make_async_copy(t_hbm, rows_buf.at[0], load_sem.at[0])
    load_v = pltpu.make_async_copy(v_hbm, rows_buf.at[6], load_sem.at[1])
    load_t.start()
    load_v.start()

    barrier = pltpu.get_barrier_semaphore()
    peers = [other] + [(block(by), q) for by in (-2, -1, 1, 2) for q in (0, 1)]
    for peer in peers:
        pl.semaphore_signal(barrier, inc=1, device_id=peer, device_id_type=MESH)
    pl.semaphore_wait(barrier, len(peers))

    scale = scale_ref[0]
    scale2 = scale * LOG2E

    def copy(slot, k):
        where = slot % 6
        is_v = slot // 6
        if where == 1:
            source, peer = slot - 1, other
        elif where == 4:
            source, peer = slot - 4, (up if is_v else down)
        elif where == 5:
            source, peer = slot - 4, (up if is_v else down)
        else:
            ahead = odd if is_v else 1 - odd
            source, peer = 6 * is_v + (where - 2) + 4 * ahead, mate
        at = pl.ds(pl.multiple_of(k * chunk, chunk), chunk)
        held = (v_hbm if is_v else t_hbm).at[at] if where in (1, 4) else rows_buf.at[source, at]
        return pltpu.make_async_remote_copy(
            held, rows_buf.at[slot, at],
            send_sem.at[slot, k], recv_sem.at[slot, k], device_id=peer, device_id_type=MESH,
        )

    def send_all(slot, first=0, last=CHUNKS):
        @pl.loop(first, last)
        def _(k):
            copy(slot, k).start()

    def arrived(slot, k):
        at = pl.ds(pl.multiple_of(k * chunk, chunk), chunk)
        pltpu.make_async_remote_copy(
            rows_buf.at[slot, at], rows_buf.at[slot, at],
            send_sem.at[1, 0], recv_sem.at[slot, k], device_id=other, device_id_type=MESH,
        ).wait_recv()

    def part_arrived(slot, part):
        @pl.loop(0, per_part)
        def _(k):
            arrived(slot, part * per_part + k)

    send_all(1)

    @pl.when(odd == 0)
    def _():
        send_all(4)

    load_t.wait()
    load_v.wait()

    @pl.when(odd == 1)
    def _():
        send_all(10)
        send_all(2)

    @pl.when(odd == 0)
    def _():
        send_all(8)

    peak[...] = jnp.full(peak.shape, LOW, jnp.float32)
    total[...] = jnp.zeros(total.shape, jnp.float32)
    acc[...] = jnp.zeros(acc.shape, jnp.float32)

    def first_events(k):
        arrived(1, k)

        @pl.when(odd == 0)
        def _():
            copy(5, k).start()

            @pl.when(k < per_part)
            def _():
                for j in range(2):
                    arrived(4, 2 * k + j)
                    copy(2, 2 * k + j).start()

            @pl.when(k >= per_part)
            def _():
                for j in range(2):
                    arrived(5, 2 * (k - per_part) + j)
                    copy(3, 2 * (k - per_part) + j).start()

            @pl.when(k == 2)
            def _():
                send_all(10)

        @pl.when(odd == 1)
        def _():
            copy(3, k).start()

            @pl.when(k < per_part)
            def _():
                for j in range(2):
                    arrived(10, 2 * k + j)
                    copy(8, 2 * k + j).start()

        @pl.when(k == CHUNKS - 2)
        def _():
            copy(7, 0).start()

        @pl.when(k == CHUNKS - 1)
        def _():
            @pl.when(odd == 1)
            def _():
                send_all(4, 0, 2)

    def half_of(part):
        return pl.ds(pl.multiple_of(part * part_rows, part_rows), part_rows)

    def product(left, slot, part):
        return (
            lax.dot_general(
                rows_buf[left], rows_buf[slot, half_of(part)], (((1,), (1,)), ((), ())),
                preferred_element_type=jnp.float32,
            )
            * scale2
        )

    @pl.loop(0, len(FIRST_EVEN))
    def _(n):
        upto, slot, part = looked_up(n, odd, FIRST_EVEN, FIRST_ODD)
        since, _, _ = looked_up(jnp.maximum(n - 1, 0), odd, FIRST_EVEN, FIRST_ODD)

        @pl.loop(since, upto)
        def _(k):
            first_events(k)

        @pl.when((slot == 2) | (slot == 3))
        def _():
            part_arrived(slot, part)

        far = jnp.where((odd == 1) & (slot >= 4), 1, 0)
        tile = product(6 + 4 * far, slot - 4 * far, part)
        scores[slot, :, half_of(part)] = tile
        before = peak[far]
        now = jnp.maximum(before, tile.max(axis=1, keepdims=True))
        peak[far] = now
        summed = jnp.exp2(tile - wide(now, part_rows)).sum(axis=1, keepdims=True)
        total[far] = total[far] * jnp.exp2(before - now) + summed
        top = tile.max(axis=0, keepdims=True)
        own_col[slot, :, half_of(part)] = top + log2(jnp.exp2(tile - top).sum(axis=0, keepdims=True))

        early = jnp.where(odd == 1, n < 6, (n < 2) | ((n >= 7) & (n < 9)))

        @pl.when(early)
        def _():
            even_slot = jnp.where(n < 2, 6, 8)
            even_part = jnp.where(n < 2, n, n - 7)
            e_slot = jnp.where(odd == 1, 6 + 2 * (n // 2), even_slot)
            e_part = jnp.where(odd == 1, n % 2, even_part)

            @pl.when(e_slot == 8)
            def _():
                part_arrived(8, e_part)

            scores[e_slot, :, half_of(e_part)] = product(0, e_slot, e_part)

    def second_events(k):
        @pl.when(k < CHUNKS)
        def _():
            arrived(7, k)
            copy(11, k).start()

            @pl.when(odd == 0)
            def _():
                copy(9, k).start()

        @pl.when((k > 0) & (odd == 1))
        def _():
            arrived(11, k - 1)
            copy(9, k - 1).start()

    label_next = (h + odd * flip_t) % 2
    label_after = (h + flip_t) % 2

    def small(source, target, sends, recvs, at, peer):
        return pltpu.make_async_remote_copy(
            source, target, sends, recvs.at[at], device_id=peer, device_id_type=MESH
        )

    @pl.when(odd == 1)
    def _():
        for slot in range(2):
            own_col[slot] = merged(own_col[slot], own_col[slot + 4])

    col_to = small(own_col.at[1], got_col.at[1], col_send.at[1], col_recv, 1, other)
    col_next = [
        small(own_col.at[2 + j], got_col.at[2 + h], col_send.at[2 + j], col_recv, 2 + h, (block(1), (label_next + j) % 2))
        for j in range(2)
    ]
    col_after = [
        small(own_col.at[4 + j], got_col.at[4 + h], col_send.at[4 + j], col_recv, 4 + h, (block(2), (label_after + j) % 2))
        for j in range(2)
    ]
    row_back = small(own_row.at[1], got_row.at[0], row_send.at[0], row_recv, 0, down)
    for each in [*col_next, col_to]:
        each.start()

    @pl.when(odd == 0)
    def _():
        for each in col_after:
            each.start()

    @pl.when(odd == 1)
    def _():
        own_row[1] = jnp.transpose(peak[1] + log2(total[1]))[:1]
        row_back.start()
        for slot in (4, 5):
            got_col[slot] = jnp.full(got_col.shape[1:], LOW, jnp.float32)

    own_row[0] = jnp.transpose(peak[0] + log2(total[0]))[:1]

    row_to = [small(lanes.at[6], lanes.at[7], lane_send.at[6], lane_recv, 7, other)]
    row_to += [
        small(lanes.at[6], lanes.at[6 + 2 * by + h], lane_send.at[5 + 2 * by + q], lane_recv, 6 + 2 * by + h, (block(by), q))
        for by in (1, 2) for q in (0, 1)
    ]

    @pl.when(odd == 0)
    def _():
        lanes[6] = own_row[0]
        for each in row_to:
            each.start()

    send_all(7, 1, 3)

    @pl.when(odd == 1)
    def _():
        send_all(4, 2, 5)

    second_events(0)

    def col_arrived(at):
        small(own_col.at[1], got_col.at[at], col_send.at[1], col_recv, at, other).wait_recv()

    for at in (1, 2, 3):
        col_arrived(at)

    @pl.when(odd == 0)
    def _():
        for at in (4, 5):
            col_arrived(at)

    terms = [own_col[0]] + [got_col[at] for at in range(1, 6)]
    top = functools.reduce(jnp.maximum, terms)
    lanes[0] = top + log2(functools.reduce(jnp.add, [jnp.exp2(term - top) for term in terms]))
    col_back = [small(lanes.at[0], lanes.at[1], lane_send.at[0], lane_recv, 1, other)]
    col_back += [
        small(lanes.at[0], lanes.at[2 * by + h], lane_send.at[2 * by - 1 + q], lane_recv, 2 * by + h, (block(-by), q))
        for by in (1, 2) for q in (0, 1)
    ]
    for each in col_back:
        each.start()

    @pl.when(odd == 1)
    def _():
        row_back.wait_recv()
        lanes[6] = merged(own_row[0], got_row[0])
        for each in row_to:
            each.start()

    send_all(7, 3)

    @pl.when(odd == 1)
    def _():
        send_all(4, 5)
        send_all(5)

    second_events(1)

    same = lax.broadcasted_iota(jnp.int32, (half, half), 0) == lax.broadcasted_iota(jnp.int32, (half, half), 1)
    diagonal[...] = jnp.where(same, scores[0], 0.0).sum(axis=0, keepdims=True)

    def spread(row):
        return jnp.transpose(jnp.broadcast_to(row, (128, half)))

    column[0] = spread(lanes[6])
    column[1] = spread(lanes[0])
    image_loss[...] = LN2 * (lanes[6] - diagonal[...])
    text_loss[...] = LN2 * (lanes[0] - diagonal[...])
    def lane_of(slot):
        where = slot % 6
        side = slot // 6
        flipped = jnp.where(side == 0, flip_t, flip_v)
        straight = (where < 4) & (odd == side)
        label = (h + jnp.where(straight, 0, flipped) + where % 2) % 2
        return jnp.where(where < 2, slot, slot - where % 2 + label)

    def finish(side, own, ref):
        @pl.loop(0, CHUNKS)
        def _(k):
            at = pl.ds(pl.multiple_of(k * chunk, chunk), chunk)
            ref[at] = scale * acc[side, at] - 2.0 * scale * rows_buf[own, at].astype(jnp.float32)


    steps = len(SECOND_EVEN)

    @pl.loop(0, steps)
    def _(n):
        upto, slot, part = looked_up(n, odd, SECOND_EVEN, SECOND_ODD)
        since, _, _ = looked_up(jnp.maximum(n - 1, 0), odd, SECOND_EVEN, SECOND_ODD)
        since = jnp.where(n == 0, 2, since)

        @pl.loop(since, upto)
        def _(k):
            second_events(k)

        side = slot // 6
        late = jnp.where(odd == 1, (slot == 4) | (slot == 5), (slot == 10) | (slot == 11))

        @pl.when(late | (slot == 9))
        def _():
            part_arrived(slot, part)

        @pl.when(late | (slot == 7) | (slot == 9) | (slot == 11))
        def _():
            scores[slot, :, half_of(part)] = product(6 * (1 - side), slot, part)

        lane = lane_of(slot)

        @pl.when((part == 0) & (slot % 6 > 0))
        def _():
            small(lanes.at[0], lanes.at[lane], lane_send.at[0], lane_recv, lane, other).wait_recv()

        tile = scores[slot, :, half_of(part)]
        weights = (
            jnp.exp2(tile - wide(column[side], part_rows)) + jnp.exp2(tile - lanes[lane, :, half_of(part)])
        ).astype(jnp.bfloat16)
        for at in range(0, width, 256):
            cols = pl.ds(at, min(256, width))
            acc[side, :, cols] += jnp.dot(
                weights, rows_buf[slot, half_of(part), cols], preferred_element_type=jnp.float32
            )

        @pl.when(n == jnp.where(odd == 1, 21, 17))
        def _():
            finish(0, 0, image_grad)

    finish(1, 6, text_grad)

    @pl.loop(0, CHUNKS)
    def _(k):
        for slot in (1, 2, 3, 4, 5, 7, 8, 9, 10, 11):
            copy(slot, k).wait_send()

    for each in [*col_next, col_to, *row_to, *col_back]:
        each.wait_send()

    @pl.when(odd == 0)
    def _():
        for each in col_after:
            each.wait_send()

    @pl.when(odd == 1)
    def _():
        row_back.wait_send()


def placed(*refs):
    half = len(refs) // 2
    sources, targets, sem = refs[:half], refs[half : 2 * half], refs[2 * half]
    copies = [pltpu.make_async_copy(a, b, sem.at[i]) for i, (a, b) in enumerate(zip(sources, targets))]
    for each in copies:
        each.start()
    for each in copies:
        each.wait()


def shards(n_dp, group, v, t, scale):
    half, width = v.shape
    f32, bf16 = jnp.float32, jnp.bfloat16
    dma = pltpu.SemaphoreType.DMA
    row = jax.ShapeDtypeStruct((1, half), f32)
    grad = jax.ShapeDtypeStruct((half, width), f32)
    near = pl.BlockSpec(memory_space=pltpu.VMEM)
    far = pl.BlockSpec(memory_space=pltpu.HBM)
    results = pl.pallas_call(
        functools.partial(kernel, n_dp, group),
        out_shape=(row, row, grad, grad),
        in_specs=[pl.BlockSpec(memory_space=pltpu.SMEM), far, far],
        out_specs=(near,) * 4,
        scratch_shapes=[
            pltpu.VMEM((12, half, width), bf16),
            pltpu.VMEM((12, half, half), f32),
            pltpu.VMEM((2, half, width), f32),
            pltpu.VMEM((2, half, 128), f32),
            pltpu.VMEM((2, half, 128), f32),
            pltpu.VMEM((6, 1, half), f32),
            pltpu.VMEM((6, 1, half), f32),
            pltpu.VMEM((2, 1, half), f32),
            pltpu.VMEM((1, 1, half), f32),
            pltpu.VMEM((12, 1, half), f32),
            pltpu.VMEM((2, half, 128), f32),
            pltpu.VMEM((1, half), f32),
            dma((12, CHUNKS)),
            dma((12, CHUNKS)),
            dma((6,)),
            dma((6,)),
            dma((1,)),
            dma((1,)),
            dma((12,)),
            dma((12,)),
            dma((2,)),
        ],
        compiler_params=pltpu.CompilerParams(
            collective_id=0, has_side_effects=True, vmem_limit_bytes=44 << 20
        ),
        cost_estimate=pl.CostEstimate(flops=13_000_000_000, bytes_accessed=6 << 20, transcendentals=10_000_000),
    )(scale, v, t)
    image_loss, text_loss, image_grad, text_grad = pl.pallas_call(
        placed,
        out_shape=(row, row, grad, grad),
        in_specs=[near] * 4,
        out_specs=(far,) * 4,
        scratch_shapes=[dma((4,))],
        compiler_params=pltpu.CompilerParams(vmem_limit_bytes=8 << 20),
    )(*results)
    return image_loss.reshape(half), text_loss.reshape(half), image_grad, text_grad


def solution(mesh):
    n_dp = mesh.shape["dp"]
    split = P(("dp", "dup"), None)
    flat = P(("dp", "dup"))
    return jax.shard_map(
        functools.partial(shards, n_dp, n_dp // 2),
        mesh=mesh,
        in_specs=(split, split, P()),
        out_specs=(flat, flat, split, split),
        check_vma=False,
    )
```
